32 devices in a mesh: freq: 8 (over z, y), pencil: 4 (over x, core).
Axes of the slice: x: 2, y: 2, z: 4, core: 2. Of those that a mesh axis runs over, the one named last changes fastest.
Arguments:
- wave_field: float32 [16, 512, 2, 512], P('freq', 'pencil'), may hold values from -6 to 6
- source_field: float32 [1, 16, 512, 2, 512], P(None, 'freq', 'pencil'), may hold values from -6 to 6
- omegas: float32 [16], P('freq'), may hold values from 30 to 250
- velocities: float32 [1, 6], replicated, may hold values from 1500 to 4500
- lower_ref: int32 [1, 8, 8], replicated, may hold values from 0 to 4, as said below
- blend_weight: float32 [1, 8, 8], replicated, may hold values from 0 to 1
Outputs:
- new_field: float32 [16, 512, 2, 512], P('freq', 'pencil')
- image: float32 [1, 512, 512], P(None, 'pencil', 'freq')
The draws below stay inside these ranges and needn't reach their ends.
Inputs may be any that keep to these rules, and one draw needn't show every extreme that they name: `lower_ref`: in each depth step the lower references of one tile row differ by at most one, so a tile row's tiles use at most three consecutive references; in each depth step one tile row uses references 0 to 2 and another references 6 - 3 to 5.
All inputs are finite; a program needn't handle non-finite values.
Results may differ from the reference program's by a relative error of at most 0.0001.
Values sent between devices are 32-bit elements; how exact they have to be, the bound alone decides.
A program may use at most 128 MiB of HBM per device.

```python
import math
import jax
import jax.numpy as jnp
from jax import lax

NX = 512
NY = 512
TILE = 64
NREF = 6
DEPTHS = 1
NW = 16
NTX = 8
NTY = 8


def draw_lower_ref(key, part):

    def one_depth(depth_key):
        key_base, key_step, key_rows = jax.random.split(depth_key, 3)
        rows_count = NX // TILE
        cols_count = NY // TILE
        base_row = jax.random.randint(key_base, (rows_count, 1), 0, NREF - 2)
        step_tile = jax.random.randint(key_step, (rows_count, cols_count), 0, 2)
        order = jax.random.permutation(key_rows, rows_count)
        row_ids = jnp.arange(rows_count)[:, None]
        col_ids = jnp.arange(cols_count)[None, :]
        base_row = jnp.where(row_ids == order[0], 0, base_row)
        base_row = jnp.where(row_ids == order[1], NREF - 3, base_row)
        forced = (row_ids == order[0]) | (row_ids == order[1])
        step_tile = jnp.where(forced & (col_ids == 0), 0, step_tile)
        step_tile = jnp.where(forced & (col_ids == 1), 1, step_tile)
        return (base_row + step_tile).astype(jnp.int32)
    return jax.vmap(one_depth)(jax.random.split(jax.random.fold_in(key, 17), DEPTHS))


def raised(array, rng, source, target, shards_of, factor):
    owner, partner = [(jnp.arange(array.shape[dim]) // (array.shape[dim] // shards_of)).reshape([-1 if axis == dim else 1 for axis in range(array.ndim)]) for dim in (source, target)]
    chosen = jax.random.permutation(rng, shards_of)[partner]
    strong = (owner == chosen) | (owner == (partner + shards_of // 2) % shards_of)
    return jnp.where(strong, factor * array, array)


def levels(rng, dims, cuts, smallest, top_value):
    loudness = 1.0
    for position, shards_of in cuts:
        steps = jax.random.uniform(jax.random.fold_in(jax.random.fold_in(rng, 6), position), (shards_of,), jnp.float32, smallest / len(cuts), top_value / len(cuts))
        loudness = loudness * jnp.repeat(jnp.exp(steps), dims[position] // shards_of).reshape((-1,) + (1,) * (len(dims) - 1 - position))
    return loudness


def noise(own_key, dims, spread, reach, cuts=(), kind=jnp.bfloat16):
    drawn = spread * jax.random.normal(own_key, dims, jnp.float32)
    if cuts:
        drawn = drawn * levels(own_key, dims, cuts, -0.22, 0.18)
    return jnp.clip(drawn, -reach, reach).astype(kind)


def gaussian_with(stream_key, extent, deviation, limit, cuts, heavy, kind=jnp.bfloat16):
    array = deviation * jax.random.normal(stream_key, extent, jnp.float32)
    if cuts:
        array = array * levels(stream_key, extent, cuts, -0.22, 0.18)
    return jnp.clip(raised(array, jax.random.fold_in(stream_key, 3), *heavy), -limit, limit).astype(kind)


def setup_inputs(seed: int = 0) -> dict:
    splits = jax.random.split(jax.random.key(seed), 7)
    wave_field = noise(splits[0], (NW, NX, 2, NY), 1.0, 6.0, ((0, 8), (1, 4)), jnp.float32)
    source_field = gaussian_with(splits[1], (DEPTHS, NW, NX, 2, NY), 1.0, 6.0, ((1, 8), (2, 4)), (1, 4, 8, 2.0), jnp.float32)
    omegas = jnp.clip(30.0 + 220.0 * jax.random.uniform(splits[2], (NW,), jnp.float32) ** levels(splits[2], (NW,), ((0, 8),), -0.2, 0.2), 30.0, 250.0)
    velocities = jnp.clip(jax.random.uniform(splits[3], (DEPTHS, NREF), jnp.float32, 1500.0, 4500.0), 1500.0, 4500.0)
    lower_ref = draw_lower_ref(jax.random.fold_in(splits[6], 71), 0)
    blend_weight = jnp.clip(jax.random.uniform(splits[5], (DEPTHS, NTX, NTY), jnp.float32, 0.0, 1.0), 0.0, 1.0)
    return {"wave_field": wave_field, "source_field": source_field, "omegas": omegas, "velocities": velocities, "lower_ref": lower_ref, "blend_weight": blend_weight}


GRID_SPACING = 12.5
DEPTH_STEP = 10.0

def wave_numbers(amount, offset, length):
    index_all = offset + jnp.arange(amount, dtype=jnp.int32)
    signed = jnp.where(index_all < length // 2, index_all, index_all - length)
    return signed.astype(jnp.float32) * (2.0 * math.pi / (length * GRID_SPACING))

def phase_terms(angular, velocity, radial):
    vertical = (angular / velocity) ** 2 - radial
    travel = jnp.sqrt(jnp.maximum(vertical, 0.0)) * DEPTH_STEP
    damping = jnp.exp(-jnp.sqrt(jnp.maximum(-vertical, 0.0)) * DEPTH_STEP)
    return (damping * jnp.cos(travel), damping * jnp.sin(travel))

def tile_coefficients(lower_idx, weight, ref_value):
    return jnp.where(lower_idx == ref_value, weight, 0.0) + jnp.where(lower_idx + 1 == ref_value, 1.0 - weight, 0.0)

def reference(wave_field, source_field, omegas, velocities, lower_ref, blend_weight):
    radial = wave_numbers(NX, 0, NX)[:, None] ** 2 + wave_numbers(NY, 0, NY)[None, :] ** 2
    wavefield = wave_field
    images = []
    image_scale = 1.0 / math.sqrt(NW)
    for depth_index in range(DEPTHS):
        lower_pix = jnp.repeat(jnp.repeat(lower_ref[depth_index], TILE, axis=0), TILE, axis=1)
        weight_pix = jnp.repeat(jnp.repeat(blend_weight[depth_index], TILE, axis=0), TILE, axis=1)
        coefficients = [tile_coefficients(lower_pix, weight_pix, ref_index) for ref_index in range(NREF)]
        speeds = velocities[depth_index]

        def extrapolate(element):
            frequency_plane, angular = element
            spectrum = jnp.fft.fft2(frequency_plane[:, 0] + 1j * frequency_plane[:, 1], norm='ortho')
            total_real = jnp.zeros((NX, NY), jnp.float32)
            total_imag = jnp.zeros((NX, NY), jnp.float32)
            for ref_index in range(NREF):
                cos_part, sin_part = phase_terms(angular, speeds[ref_index], radial)
                shifted = jnp.fft.ifft2(spectrum * (cos_part + 1j * sin_part), norm='ortho')
                total_real = total_real + coefficients[ref_index] * jnp.real(shifted)
                total_imag = total_imag + coefficients[ref_index] * jnp.imag(shifted)
            return jnp.stack([total_real, total_imag], axis=1)
        wavefield = lax.map(extrapolate, (wavefield, omegas))
        source = source_field[depth_index]
        depth_image = lax.optimization_barrier(jnp.sum(source[:, :, 0] * wavefield[:, :, 0] + source[:, :, 1] * wavefield[:, :, 1], axis=0)) * image_scale
        images.append(depth_image)
    return (wavefield, jnp.stack(images))
```

```python
import functools
import math

import jax
import jax.numpy as jnp
import ml_dtypes
import numpy as np
from jax import lax
from jax.experimental import pallas as pl
from jax.experimental.pallas import tpu as pltpu
from jax.sharding import PartitionSpec as P

GRID_SPACING = 12.5
DEPTH_STEP = 10.0
MESH = pl.DeviceIdType.MESH


def real_tables(length):
    half, quarter = length // 2, length // 4
    points = np.arange(half)
    out = []
    for parity in (0, 1):
        waves = 2 * np.arange(quarter) + parity
        angles = 2.0 * np.pi * ((waves[:, None] * points[None, :]) % length) / length
        cosines = np.cos(angles) * math.sqrt(2.0 / length)
        sines = np.sin(angles) * math.sqrt(2.0 / length)
        if parity == 0:
            cosines[0] = 1.0 / math.sqrt(length)
            sines[0] = np.where(points % 2 == 0, 1.0, -1.0) / math.sqrt(length)
        out.append(np.concatenate([cosines, sines]))
    table = np.stack(out)
    both = np.stack([table, table.transpose(0, 2, 1)])
    high = both.astype(ml_dtypes.bfloat16)
    low = (both - high.astype(np.float64)).astype(ml_dtypes.bfloat16)
    return high, low


def halves(values):
    high = values.astype(jnp.bfloat16)
    low = (values - high.astype(jnp.float32)).astype(jnp.bfloat16)
    return high, low


def dot(a, b):
    return jnp.dot(a, b, preferred_element_type=jnp.float32)


def product(a, b):
    return dot(a[0], b[0]) + (dot(a[0], b[1]) + dot(a[1], b[0]))


def kernel(
    dims,
    wave_ref,
    source_ref,
    high_x,
    low_x,
    high_y,
    low_y,
    omega_ref,
    speed_ref,
    lower_ref,
    weight_ref,
    out_ref,
    image_ref,
    stage,
    recv,
    phase,
    shifted,
    coef,
    blend_own,
    blend_recv,
    img_send,
    img_recv,
    send_sem,
    recv_sem,
    pair_send,
    pair_recv,
    isend_sem,
    irecv_sem,
):
    freqs, pencils, groups, rows, width_x, width_y, refs, tile, scale = dims
    chips = pencils // 2
    half_x, half_y = width_x // 2, width_y // 2
    quarter_x, quarter_y = width_x // 4, width_y // 4
    band = 2 * rows
    me = lax.axis_index("pencil")
    group = lax.axis_index("freq")
    core = lax.rem(me, 2)
    chip = lax.div(me, 2)
    partner = chip * 2 + (1 - core)

    barrier = pltpu.get_barrier_semaphore()
    for step in range(1, pencils):
        pl.semaphore_signal(
            barrier, inc=1, device_id=(group, lax.rem(me + step, pencils)), device_id_type=MESH
        )
    for step in range(1, groups):
        pl.semaphore_signal(
            barrier, inc=1, device_id=(lax.rem(group + step, groups), me), device_id_type=MESH
        )

    sends = []
    for f in range(freqs):
        for c in range(2):
            values = wave_ref[f, c]
            first, second = values[:, :half_y], values[:, half_y:]
            for e in range(2):
                mixed = first + second if e == 0 else first - second
                stage[f, e, c] = product(halves(mixed), (high_y[1, e], low_y[1, e]))
        recv[f, me] = stage[f, core]
        if f == 0:
            pl.semaphore_wait(barrier, pencils - 1 + groups - 1)
        for far in list(range(1, chips)) + [0]:
            for flip in range(2):
                if far == 0 and flip == 0:
                    continue
                to_core = (core + flip) % 2
                slot = far * 2 + flip
                target = lax.rem(chip + far, chips) * 2 + to_core
                copy = pltpu.make_async_remote_copy(
                    src_ref=stage.at[f, to_core],
                    dst_ref=recv.at[f, me],
                    send_sem=send_sem.at[f, slot],
                    recv_sem=recv_sem.at[f, slot],
                    device_id=(group, target),
                    device_id_type=MESH,
                )
                copy.start()
                sends.append((f, copy))

    tile_rows = band // tile
    tiles_y = width_y // tile
    lane_y = lax.broadcasted_iota(jnp.int32, (8, width_y), 1)
    bases = []
    for t in range(tile_rows):
        row = chip * tile_rows + t
        lowers = [lower_ref[row, q] for q in range(tiles_y)]
        base = functools.reduce(jnp.minimum, lowers)
        base = jnp.minimum(base, refs - 3)
        bases.append(base)
        for k in range(3):
            line = jnp.zeros((8, width_y), jnp.float32)
            for q in range(tiles_y):
                w = weight_ref[row, q]
                value = jnp.where(lowers[q] == base + k, w, 0.0) + jnp.where(
                    lowers[q] + 1 == base + k, 1.0 - w, 0.0
                )
                line = jnp.where((lane_y >= q * tile) & (lane_y < (q + 1) * tile), value, line)
            coef[t, k] = line

    step_x = 2.0 * math.pi / (width_x * GRID_SPACING)
    step_y = 2.0 * math.pi / (width_y * GRID_SPACING)

    def terms(angular, velocity, radial):
        vertical = (angular / velocity) ** 2 - radial
        travel = jnp.sqrt(jnp.maximum(vertical, 0.0)) * DEPTH_STEP
        damping = jnp.exp(-jnp.sqrt(jnp.maximum(-vertical, 0.0)) * DEPTH_STEP)
        return damping * jnp.cos(travel), damping * jnp.sin(travel)

    lanes = lax.broadcasted_iota(jnp.int32, (1, quarter_y), 1)
    ky = (2 * lanes + core).astype(jnp.float32) * step_y
    ky_extra = jnp.where(core == 0, half_y, 1).astype(jnp.float32) * step_y
    even_rows = 2 * lax.broadcasted_iota(jnp.int32, (quarter_x, 1), 0)
    kx_even = even_rows.astype(jnp.float32) * step_x
    kx_odd = (even_rows + 1).astype(jnp.float32) * step_x
    kx_last = jnp.full((8, 1), half_x, jnp.int32).astype(jnp.float32) * step_x
    row_id = lax.broadcasted_iota(jnp.int32, (quarter_x, quarter_y), 0)
    lane_id = lax.broadcasted_iota(jnp.int32, (quarter_x, quarter_y), 1)
    speeds_row = jnp.full((1, quarter_y), speed_ref[0, 0], jnp.float32)
    for r in range(1, refs):
        speeds_row = jnp.where(lanes == r, speed_ref[0, r], speeds_row)

    for f in range(freqs):
        angular = omega_ref[f]
        extra = [
            terms(angular, speeds_row, kx * kx + ky_extra * ky_extra)
            for kx in (kx_even, kx_last, kx_odd)
        ]
        for r in range(refs):
            velocity = speed_ref[0, r]
            main = [
                terms(angular, velocity, kx * kx + ky * ky) for kx in (kx_even, kx_last, kx_odd)
            ]
            for part in range(2):
                even, last, odd = (m[part] for m in main)
                even_x, last_x, odd_x = (m[part][:, r : r + 1] for m in extra)
                even_s = jnp.where(row_id == 0, last[0:1], even)
                even_sx = jnp.where(row_id[:, 0:1] == 0, last_x[0:1], even_x)
                blocks = ((even, even_x), (even_s, even_sx), (odd, odd_x), (odd, odd_x))
                for i, (block, column) in enumerate(blocks):
                    span = slice(i * quarter_x, (i + 1) * quarter_x)
                    phase[f, r, part, span, :quarter_y] = block
                    phase[f, r, part, span, quarter_y:] = jnp.where(lane_id == 0, column, block)

    start = lax.rem(chip * band, half_x)
    sign_x = jnp.where(chip * band < half_x, 1.0, -1.0)
    sign_y = jnp.where(core == 0, 1.0, -1.0)
    start = pl.multiple_of(start, rows)
    back = [
        (high_x[1, e, pl.ds(start, band), :], low_x[1, e, pl.ds(start, band), :]) for e in range(2)
    ]
    table_y = (high_y[0, core], low_y[0, core])

    pair_copies = []
    for f in range(freqs):
        for g, copy in sends:
            if g == f:
                copy.wait_recv()
        spectrum = []
        for c in range(2):
            upper = recv[f, 0 : pencils // 2, c].reshape(half_x, half_y)
            lower = recv[f, pencils // 2 : pencils, c].reshape(half_x, half_y)
            even = product((high_x[0, 0], low_x[0, 0]), halves(upper + lower))
            odd = product((high_x[0, 1], low_x[0, 1]), halves(upper - lower))
            spectrum.append((even, odd))

        def one_ref(r, carry):
            total = [None, None]
            for e in range(2):
                span = slice(e * half_x, (e + 1) * half_x)
                real, imag = spectrum[0][e], spectrum[1][e]
                pc, ps = phase[f, r, 0, span, :], phase[f, r, 1, span, :]
                moved = (real * pc - imag * ps, real * ps + imag * pc)
                for c in range(2):
                    share = product(back[e], halves(moved[c]))
                    total[c] = share if e == 0 else total[c] + sign_x * share
            for c in range(2):
                shifted[r, c] = total[c]
            return carry

        for r in range(refs):
            one_ref(r, 0)

        for t in range(tile_rows):
            lo, hi = [None, None], [None, None]
            for k in range(3):
                block = shifted[bases[t] + k, :, t * tile : (t + 1) * tile, :]
                space = product(halves(block.reshape(2 * tile, half_y)), table_y)
                for c in range(2):
                    piece = space[c * tile : (c + 1) * tile]
                    a = coef[t, k, 0:1, :half_y] * piece
                    b = coef[t, k, 0:1, half_y:] * piece
                    lo[c] = a if k == 0 else lo[c] + a
                    hi[c] = b if k == 0 else hi[c] + b
            owner, inner = (t * tile) // rows, (t * tile) % rows
            for c in range(2):
                blend_own[f, owner, c, inner : inner + tile, :half_y] = lo[c]
                blend_own[f, owner, c, inner : inner + tile, half_y:] = hi[c] * sign_y
        copy = pltpu.make_async_remote_copy(
            src_ref=blend_own.at[f, 1 - core],
            dst_ref=blend_recv.at[f],
            send_sem=pair_send.at[f],
            recv_sem=pair_recv.at[f],
            device_id=(group, partner),
            device_id_type=MESH,
        )
        copy.start()
        pair_copies.append(copy)

    image = None
    for f in range(freqs):
        pair_copies[f].wait_recv()
        for c in range(2):
            value = blend_own[f, core, c] + blend_recv[f, c]
            out_ref[f, c] = value
            term = source_ref[f, c] * value
            image = term if image is None else image + term
    image = image * scale

    own_width = width_y // groups
    packs = 128 // own_width
    chunk = rows // packs
    lane = lax.broadcasted_iota(jnp.int32, (chunk, 128), 1)
    for g in range(groups):
        at = g * own_width
        column = image[:, at // 128 * 128 : at // 128 * 128 + 128]
        offset = at % 128
        packed = None
        for i in range(packs):
            part = column[i * chunk : (i + 1) * chunk]
            shift = (i * own_width - offset) % 128
            if shift:
                part = pltpu.roll(part, shift, 1)
            packed = part if packed is None else jnp.where(lane >= i * own_width, part, packed)
        img_send[g] = packed
    image_copies = []
    for step in range(1, groups):
        to = lax.rem(group + step, groups)
        copy = pltpu.make_async_remote_copy(
            src_ref=img_send.at[to],
            dst_ref=img_recv.at[step],
            send_sem=isend_sem.at[step],
            recv_sem=irecv_sem.at[step],
            device_id=(to, me),
            device_id_type=MESH,
        )
        copy.start()
        image_copies.append(copy)
    total = img_send[group]
    for step, copy in enumerate(image_copies):
        copy.wait_recv()
        total = total + img_recv[step + 1]
    for i in range(packs):
        part = pltpu.roll(total, (-i * own_width) % 128, 1) if i else total
        image_ref[i * chunk : (i + 1) * chunk, :] = part[:, :own_width]

    for _, copy in sends:
        copy.wait_send()
    for copy in pair_copies:
        copy.wait_send()
    for copy in image_copies:
        copy.wait_send()


def on_device(wave_field, source_field, omegas, velocities, lower_ref, blend_weight):
    pencils = lax.axis_size("pencil")
    groups = lax.axis_size("freq")
    freqs, rows, _, width_y = wave_field.shape
    width_x = rows * pencils
    refs = velocities.shape[1]
    tile = width_x // lower_ref.shape[1]
    half_y = width_y // 2
    scale = 1.0 / math.sqrt(freqs * groups)
    dims = (freqs, pencils, groups, rows, width_x, width_y, refs, tile, scale)
    own_width = width_y // groups
    tables = [jnp.asarray(t) for t in real_tables(width_x) + real_tables(width_y)]
    wave = jnp.transpose(wave_field, (0, 2, 1, 3))
    source = jnp.transpose(source_field[0], (0, 2, 1, 3))
    vmem = pl.BlockSpec(memory_space=pltpu.VMEM)
    smem = pl.BlockSpec(memory_space=pltpu.SMEM)
    f32 = jnp.float32
    packed = (groups, rows * own_width // 128, 128)
    out, image = pl.pallas_call(
        functools.partial(kernel, dims),
        out_shape=(
            jax.ShapeDtypeStruct((freqs, 2, rows, width_y), f32),
            jax.ShapeDtypeStruct((rows, own_width), f32),
        ),
        in_specs=[vmem] * 6 + [smem] * 4,
        out_specs=(vmem, vmem),
        scratch_shapes=[
            pltpu.VMEM((freqs, 2, 2, rows, half_y), f32),
            pltpu.VMEM((freqs, pencils, 2, rows, half_y), f32),
            pltpu.VMEM((freqs, refs, 2, width_x, half_y), f32),
            pltpu.VMEM((refs, 2, 2 * rows, half_y), f32),
            pltpu.VMEM((2 * rows // tile, 3, 8, width_y), f32),
            pltpu.VMEM((freqs, 2, 2, rows, width_y), f32),
            pltpu.VMEM((freqs, 2, rows, width_y), f32),
            pltpu.VMEM(packed, f32),
            pltpu.VMEM(packed, f32),
            pltpu.SemaphoreType.DMA((freqs, pencils)),
            pltpu.SemaphoreType.DMA((freqs, pencils)),
            pltpu.SemaphoreType.DMA((freqs,)),
            pltpu.SemaphoreType.DMA((freqs,)),
            pltpu.SemaphoreType.DMA((groups,)),
            pltpu.SemaphoreType.DMA((groups,)),
        ],
        compiler_params=pltpu.CompilerParams(
            collective_id=0, has_side_effects=True, vmem_limit_bytes=56 * 1024 * 1024
        ),
    )(wave, source, *tables, omegas, velocities, lower_ref[0], blend_weight[0])
    return jnp.transpose(out, (0, 2, 1, 3)), image[None]


def solution(mesh):
    placed = (
        P("freq", "pencil", None, None),
        P(None, "freq", "pencil", None, None),
        P("freq"),
        P(),
        P(),
        P(),
    )
    return jax.shard_map(
        on_device,
        mesh=mesh,
        in_specs=placed,
        out_specs=(P("freq", "pencil", None, None), P(None, "pencil", "freq")),
        check_vma=False,
    )
```

```python
import functools
import math

import jax
import jax.numpy as jnp
import ml_dtypes
import numpy as np
from jax import lax
from jax.experimental import pallas as pl
from jax.experimental.pallas import tpu as pltpu
from jax.sharding import PartitionSpec as P

GRID_SPACING = 12.5
DEPTH_STEP = 10.0
MESH = pl.DeviceIdType.MESH


def real_tables(length):
    half, quarter = length // 2, length // 4
    points = np.arange(half)
    out = []
    for parity in (0, 1):
        waves = 2 * np.arange(quarter) + parity
        angles = 2.0 * np.pi * ((waves[:, None] * points[None, :]) % length) / length
        cosines = np.cos(angles) * math.sqrt(2.0 / length)
        sines = np.sin(angles) * math.sqrt(2.0 / length)
        if parity == 0:
            cosines[0] = 1.0 / math.sqrt(length)
            sines[0] = np.where(points % 2 == 0, 1.0, -1.0) / math.sqrt(length)
        out.append(np.concatenate([cosines, sines]))
    table = np.stack(out)
    both = np.stack([table, table.transpose(0, 2, 1)])
    high = both.astype(ml_dtypes.bfloat16)
    low = (both - high.astype(np.float64)).astype(ml_dtypes.bfloat16)
    return high, low


def halves(values):
    high = values.astype(jnp.bfloat16)
    low = (values - high.astype(jnp.float32)).astype(jnp.bfloat16)
    return high, low


def dot(a, b):
    return jnp.dot(a, b, preferred_element_type=jnp.float32)


def product(a, b):
    return dot(a[0], b[0]) + (dot(a[0], b[1]) + dot(a[1], b[0]))


def kernel(
    dims,
    wave_ref,
    source_ref,
    high_fwd,
    low_fwd,
    high_x_ref,
    low_x_ref,
    high_back_ref,
    low_back_ref,
    omega_ref,
    speed_ref,
    lower_ref,
    weight_ref,
    out_ref,
    image_ref,
    stage,
    recv,
    phase,
    shifted,
    coef,
    blend_own,
    blend_send,
    blend_recv,
    img_acc,
    img_send,
    img_recv,
    wave_buf,
    source_buf,
    out_buf,
    high_x,
    low_x,
    high_back,
    low_back,
    table_sem,
    load_sem,
    store_sem,
    send_sem,
    recv_sem,
    pair_send,
    pair_recv,
    isend_sem,
    irecv_sem,
):
    freqs, pencils, groups, rows, width_x, width_y, refs, tile, scale = dims
    chips = pencils // 2
    half_x, half_y = width_x // 2, width_y // 2
    quarter_x, quarter_y = width_x // 4, width_y // 4
    band = 2 * rows
    me = lax.axis_index("pencil")
    group = lax.axis_index("freq")
    core = lax.rem(me, 2)
    chip = lax.div(me, 2)
    partner = chip * 2 + (1 - core)

    per = rows // tile
    loads = {}
    for kind, (ref, buf) in enumerate(((wave_ref, wave_buf), (source_ref, source_buf))):
        for f in range(freqs):
            for c in range(2):
                src = ref.at[f, :, c, :] if kind == 0 else ref.at[0, f, :, c, :]
                copy = pltpu.make_async_copy(src, buf.at[f, c], load_sem.at[kind, f, c])
                copy.start()
                loads[kind, f, c] = copy

    tables = []
    for i, (ref, buf) in enumerate(
        ((high_x_ref, high_x), (low_x_ref, low_x), (high_back_ref, high_back), (low_back_ref, low_back))
    ):
        copy = pltpu.make_async_copy(ref, buf, table_sem.at[i])
        copy.start()
        tables.append(copy)

    barrier = pltpu.get_barrier_semaphore()
    for step in range(1, pencils):
        pl.semaphore_signal(
            barrier, inc=1, device_id=(group, lax.rem(me + step, pencils)), device_id_type=MESH
        )
    for step in range(1, groups):
        pl.semaphore_signal(
            barrier, inc=1, device_id=(lax.rem(group + step, groups), me), device_id_type=MESH
        )

    sends = []
    for f in range(freqs):
        for c in range(2):
            loads[0, f, c].wait()
            values = wave_buf[f, c]
            first, second = values[:, :half_y], values[:, half_y:]
            for flip in (1, 0):
                to_core = lax.rem(core + flip, 2)
                sign = jnp.where(to_core == 0, 1.0, -1.0)
                mixed = halves(first + sign * second)
                piece = product(mixed, (high_fwd[to_core], low_fwd[to_core]))
                stage[f, c, flip] = piece
                if flip == 0:
                    recv[f, me, c] = piece
                if f == 0 and c == 0 and flip == 1:
                    pl.semaphore_wait(barrier, pencils - 1 + groups - 1)
                for far in list(range(1, chips)) + [0]:
                    if far == 0 and flip == 0:
                        continue
                    slot = far * 2 + flip
                    target = lax.rem(chip + far, chips) * 2 + to_core
                    copy = pltpu.make_async_remote_copy(
                        src_ref=stage.at[f, c, flip],
                        dst_ref=recv.at[f, me, c],
                        send_sem=send_sem.at[f, c, slot],
                        recv_sem=recv_sem.at[f, c, slot],
                        device_id=(group, target),
                        device_id_type=MESH,
                    )
                    copy.start()
                    sends.append((f, c, copy))

    tile_rows = band // tile
    tiles_y = width_y // tile
    lane_y = lax.broadcasted_iota(jnp.int32, (8, width_y), 1)
    bases, offsets = [], []
    for t in range(tile_rows):
        owner = 1 - core if t < per else core
        row = chip * tile_rows + owner * per + t % per
        offsets.append(pl.multiple_of(owner * rows + (t % per) * tile, tile))
        lowers = [lower_ref[row, q] for q in range(tiles_y)]
        base = functools.reduce(jnp.minimum, lowers)
        base = jnp.minimum(base, refs - 3)
        bases.append(base)
        for k in range(3):
            line = jnp.zeros((8, width_y), jnp.float32)
            for q in range(tiles_y):
                w = weight_ref[row, q]
                value = jnp.where(lowers[q] == base + k, w, 0.0) + jnp.where(
                    lowers[q] + 1 == base + k, 1.0 - w, 0.0
                )
                line = jnp.where((lane_y >= q * tile) & (lane_y < (q + 1) * tile), value, line)
            coef[t, k] = line

    step_x = 2.0 * math.pi / (width_x * GRID_SPACING)
    step_y = 2.0 * math.pi / (width_y * GRID_SPACING)

    def terms(angular, velocity, radial):
        vertical = (angular / velocity) ** 2 - radial
        travel = jnp.sqrt(jnp.maximum(vertical, 0.0)) * DEPTH_STEP
        damping = jnp.exp(-jnp.sqrt(jnp.maximum(-vertical, 0.0)) * DEPTH_STEP)
        return damping * jnp.cos(travel), damping * jnp.sin(travel)

    lanes = lax.broadcasted_iota(jnp.int32, (1, quarter_y), 1)
    ky = (2 * lanes + core).astype(jnp.float32) * step_y
    ky_extra = jnp.where(core == 0, half_y, 1).astype(jnp.float32) * step_y
    even_rows = 2 * lax.broadcasted_iota(jnp.int32, (quarter_x, 1), 0)
    kx_even = even_rows.astype(jnp.float32) * step_x
    kx_odd = (even_rows + 1).astype(jnp.float32) * step_x
    kx_last = jnp.full((8, 1), half_x, jnp.int32).astype(jnp.float32) * step_x
    row_id = lax.broadcasted_iota(jnp.int32, (quarter_x, quarter_y), 0)
    lane_id = lax.broadcasted_iota(jnp.int32, (quarter_x, quarter_y), 1)
    speeds_row = jnp.full((1, quarter_y), speed_ref[0, 0], jnp.float32)
    for r in range(1, refs):
        speeds_row = jnp.where(lanes == r, speed_ref[0, r], speeds_row)

    for f in range(freqs):
        angular = omega_ref[f]
        extra = [
            terms(angular, speeds_row, kx * kx + ky_extra * ky_extra)
            for kx in (kx_even, kx_last, kx_odd)
        ]
        for r in range(refs):
            velocity = speed_ref[0, r]
            main = [
                terms(angular, velocity, kx * kx + ky * ky) for kx in (kx_even, kx_last, kx_odd)
            ]
            for part in range(2):
                even, last, odd = (m[part] for m in main)
                even_x, last_x, odd_x = (m[part][:, r : r + 1] for m in extra)
                even_s = jnp.where(row_id == 0, last[0:1], even)
                even_sx = jnp.where(row_id[:, 0:1] == 0, last_x[0:1], even_x)
                blocks = ((even, even_x), (even_s, even_sx), (odd, odd_x), (odd, odd_x))
                for i, (block, column) in enumerate(blocks):
                    span = slice(i * quarter_x, (i + 1) * quarter_x)
                    phase[f, r, part, span, :quarter_y] = block
                    phase[f, r, part, span, quarter_y:] = jnp.where(lane_id == 0, column, block)

    for copy in tables:
        copy.wait()
    start = lax.rem(chip * band, half_x)
    sign_x = jnp.where(chip * band < half_x, 1.0, -1.0)
    sign_y = jnp.where(core == 0, 1.0, -1.0)
    start = pl.multiple_of(start, rows)
    back = [
        (high_x[1, e, pl.ds(start, band), :], low_x[1, e, pl.ds(start, band), :]) for e in range(2)
    ]
    table_y = (high_back[core], low_back[core])

    own_width = width_y // groups
    packs = 128 // own_width
    chunk = tile // packs
    lane = lax.broadcasted_iota(jnp.int32, (chunk, 128), 1)
    pair_copies, stores, image_copies = [], [], []

    def finish(f):
        last = f == freqs - 1
        for i in range(per):
            span = slice(i * tile, (i + 1) * tile)
            pair_copies[f * per + i].wait_recv()
            image = None
            for c in range(2):
                value = blend_own[f, c, span] + blend_recv[f, i, c]
                out_buf[f, c, span] = value
                if i == 0:
                    loads[1, f, c].wait()
                term = source_buf[f, c, span] * value
                image = term if image is None else image + term
            if f > 0:
                image = image + img_acc[span]
            if not last:
                img_acc[span] = image
                continue
            image = image * scale
            for g in range(groups):
                at = g * own_width
                column = image[:, at // 128 * 128 : at // 128 * 128 + 128]
                packed = None
                for j in range(packs):
                    part = column[j * chunk : (j + 1) * chunk]
                    shift = (j * own_width - at) % 128
                    if shift:
                        part = pltpu.roll(part, shift, 1)
                    packed = part if packed is None else jnp.where(lane >= j * own_width, part, packed)
                img_send[i, g] = packed
            for step in range(1, groups):
                to = lax.rem(group + step, groups)
                copy = pltpu.make_async_remote_copy(
                    src_ref=img_send.at[i, to],
                    dst_ref=img_recv.at[i, step],
                    send_sem=isend_sem.at[i, step],
                    recv_sem=irecv_sem.at[i, step],
                    device_id=(to, me),
                    device_id_type=MESH,
                )
                copy.start()
                image_copies.append((i, step, copy))
        for c in range(2):
            copy = pltpu.make_async_copy(out_buf.at[f, c], out_ref.at[f, :, c, :], store_sem.at[f, c])
            copy.start()
            stores.append(copy)

    for f in range(freqs):
        if f > 0:
            finish(f - 1)
        spectrum = []
        for c in range(2):
            for g, d, copy in sends:
                if (g, d) == (f, c):
                    copy.wait_recv()
            upper = recv[f, 0 : pencils // 2, c].reshape(half_x, half_y)
            lower = recv[f, pencils // 2 : pencils, c].reshape(half_x, half_y)
            even = product((high_x[0, 0], low_x[0, 0]), halves(upper + lower))
            odd = product((high_x[0, 1], low_x[0, 1]), halves(upper - lower))
            spectrum.append((even, odd))

        def one_ref(r, carry):
            total = [None, None]
            for e in range(2):
                span = slice(e * half_x, (e + 1) * half_x)
                real, imag = spectrum[0][e], spectrum[1][e]
                pc, ps = phase[f, r, 0, span, :], phase[f, r, 1, span, :]
                moved = (real * pc - imag * ps, real * ps + imag * pc)
                for c in range(2):
                    share = product(back[e], halves(moved[c]))
                    total[c] = share if e == 0 else total[c] + sign_x * share
            for c in range(2):
                shifted[r, c] = total[c]
            return carry

        for r in range(refs):
            one_ref(r, 0)

        for t in range(tile_rows):
            lo, hi = [None, None], [None, None]
            for k in range(3):
                block = shifted[bases[t] + k, :, pl.ds(offsets[t], tile), :]
                space = product(halves(block.reshape(2 * tile, half_y)), table_y)
                for c in range(2):
                    piece = space[c * tile : (c + 1) * tile]
                    a = coef[t, k, 0:1, :half_y] * piece
                    b = coef[t, k, 0:1, half_y:] * piece
                    lo[c] = a if k == 0 else lo[c] + a
                    hi[c] = b if k == 0 else hi[c] + b
            inner = (t % per) * tile
            for c in range(2):
                if t < per:
                    blend_send[f, t, c, :, :half_y] = lo[c]
                    blend_send[f, t, c, :, half_y:] = hi[c] * sign_y
                else:
                    blend_own[f, c, inner : inner + tile, :half_y] = lo[c]
                    blend_own[f, c, inner : inner + tile, half_y:] = hi[c] * sign_y
            if t < per:
                copy = pltpu.make_async_remote_copy(
                    src_ref=blend_send.at[f, t],
                    dst_ref=blend_recv.at[f, t],
                    send_sem=pair_send.at[f, t],
                    recv_sem=pair_recv.at[f, t],
                    device_id=(group, partner),
                    device_id_type=MESH,
                )
                copy.start()
                pair_copies.append(copy)
    finish(freqs - 1)

    lines = []
    for i in range(per):
        total = img_send[i, group]
        for j, step, copy in image_copies:
            if j == i:
                copy.wait_recv()
                total = total + img_recv[i, step]
        for j in range(packs):
            part = pltpu.roll(total, (-j * own_width) % 128, 1) if j else total
            lines.append(part[:, :own_width])
    image_ref[...] = jnp.concatenate(lines, axis=0).T

    for copy in stores:
        copy.wait()
    for _, _, copy in sends:
        copy.wait_send()
    for copy in pair_copies:
        copy.wait_send()
    for _, _, copy in image_copies:
        copy.wait_send()


def on_device(wave_field, source_field, omegas, velocities, lower_ref, blend_weight):
    pencils = lax.axis_size("pencil")
    groups = lax.axis_size("freq")
    freqs, rows, _, width_y = wave_field.shape
    width_x = rows * pencils
    refs = velocities.shape[1]
    tile = width_x // lower_ref.shape[1]
    half_y = width_y // 2
    scale = 1.0 / math.sqrt(freqs * groups)
    dims = (freqs, pencils, groups, rows, width_x, width_y, refs, tile, scale)
    own_width = width_y // groups
    high_x, low_x = real_tables(width_x)
    high_y, low_y = real_tables(width_y)
    tables = [jnp.asarray(t) for t in (high_y[1], low_y[1], high_x, low_x, high_y[0], low_y[0])]
    hbm = pl.BlockSpec(memory_space=pl.ANY)
    vmem = pl.BlockSpec(memory_space=pltpu.VMEM)
    smem = pl.BlockSpec(memory_space=pltpu.SMEM)
    f32 = jnp.float32
    per = rows // tile
    packed = (per, groups, tile * own_width // 128, 128)
    out, image = pl.pallas_call(
        functools.partial(kernel, dims),
        out_shape=(
            jax.ShapeDtypeStruct(wave_field.shape, f32),
            jax.ShapeDtypeStruct((own_width, rows), f32),
        ),
        in_specs=[hbm] * 2 + [vmem] * 2 + [hbm] * 4 + [smem] * 4,
        out_specs=(hbm, vmem),
        scratch_shapes=[
            pltpu.VMEM((freqs, 2, 2, rows, half_y), f32),
            pltpu.VMEM((freqs, pencils, 2, rows, half_y), f32),
            pltpu.VMEM((freqs, refs, 2, width_x, half_y), f32),
            pltpu.VMEM((refs, 2, 2 * rows, half_y), f32),
            pltpu.VMEM((2 * per, 3, 8, width_y), f32),
            pltpu.VMEM((freqs, 2, rows, width_y), f32),
            pltpu.VMEM((freqs, per, 2, tile, width_y), f32),
            pltpu.VMEM((freqs, per, 2, tile, width_y), f32),
            pltpu.VMEM((rows, width_y), f32),
            pltpu.VMEM(packed, f32),
            pltpu.VMEM(packed, f32),
            pltpu.VMEM((freqs, 2, rows, width_y), f32),
            pltpu.VMEM((freqs, 2, rows, width_y), f32),
            pltpu.VMEM((freqs, 2, rows, width_y), f32),
            pltpu.VMEM(high_x.shape, jnp.bfloat16),
            pltpu.VMEM(high_x.shape, jnp.bfloat16),
            pltpu.VMEM(high_y.shape[1:], jnp.bfloat16),
            pltpu.VMEM(high_y.shape[1:], jnp.bfloat16),
            pltpu.SemaphoreType.DMA((4,)),
            pltpu.SemaphoreType.DMA((2, freqs, 2)),
            pltpu.SemaphoreType.DMA((freqs, 2)),
            pltpu.SemaphoreType.DMA((freqs, 2, pencils)),
            pltpu.SemaphoreType.DMA((freqs, 2, pencils)),
            pltpu.SemaphoreType.DMA((freqs, per)),
            pltpu.SemaphoreType.DMA((freqs, per)),
            pltpu.SemaphoreType.DMA((per, groups)),
            pltpu.SemaphoreType.DMA((per, groups)),
        ],
        compiler_params=pltpu.CompilerParams(
            collective_id=0, has_side_effects=True, vmem_limit_bytes=56 * 1024 * 1024
        ),
    )(wave_field, source_field, *tables, omegas, velocities, lower_ref[0], blend_weight[0])
    return out, image.T[None]


def solution(mesh):
    placed = (
        P("freq", "pencil", None, None),
        P(None, "freq", "pencil", None, None),
        P("freq"),
        P(),
        P(),
        P(),
    )
    return jax.shard_map(
        on_device,
        mesh=mesh,
        in_specs=placed,
        out_specs=(P("freq", "pencil", None, None), P(None, "pencil", "freq")),
        check_vma=False,
    )
```

```python
import functools
import math

import jax
import jax.numpy as jnp
import ml_dtypes
import numpy as np
from jax import lax
from jax.experimental import pallas as pl
from jax.experimental.pallas import tpu as pltpu
from jax.sharding import PartitionSpec as P

GRID_SPACING = 12.5
DEPTH_STEP = 10.0
MESH = pl.DeviceIdType.MESH


def real_tables(length):
    half, quarter = length // 2, length // 4
    points = np.arange(half)
    out = []
    for parity in (0, 1):
        waves = 2 * np.arange(quarter) + parity
        angles = 2.0 * np.pi * ((waves[:, None] * points[None, :]) % length) / length
        cosines = np.cos(angles) * math.sqrt(2.0 / length)
        sines = np.sin(angles) * math.sqrt(2.0 / length)
        if parity == 0:
            cosines[0] = 1.0 / math.sqrt(length)
            sines[0] = np.where(points % 2 == 0, 1.0, -1.0) / math.sqrt(length)
        out.append(np.concatenate([cosines, sines]))
    table = np.stack(out)
    both = np.stack([table, table.transpose(0, 2, 1)])
    high = both.astype(ml_dtypes.bfloat16)
    low = (both - high.astype(np.float64)).astype(ml_dtypes.bfloat16)
    return high, low


def halves(values):
    high = values.astype(jnp.bfloat16)
    low = (values - high.astype(jnp.float32)).astype(jnp.bfloat16)
    return high, low


def dot(a, b):
    return jnp.dot(a, b, preferred_element_type=jnp.float32)


def product(a, b):
    return dot(a[0], b[0]) + (dot(a[0], b[1]) + dot(a[1], b[0]))


def kernel(
    dims,
    wave_ref,
    source_ref,
    high_fwd,
    low_fwd,
    high_x_ref,
    low_x_ref,
    high_back_ref,
    low_back_ref,
    omega_ref,
    speed_ref,
    lower_ref,
    weight_ref,
    out_ref,
    image_ref,
    stage,
    recv,
    phase,
    shifted,
    coef,
    blend_own,
    blend_send,
    blend_recv,
    img_acc,
    img_send,
    img_recv,
    wave_buf,
    source_buf,
    out_buf,
    high_x,
    low_x,
    high_back,
    low_back,
    table_sem,
    load_sem,
    store_sem,
    send_sem,
    recv_sem,
    pair_send,
    pair_recv,
    isend_sem,
    irecv_sem,
):
    freqs, pencils, groups, rows, width_x, width_y, refs, tile, scale = dims
    chips = pencils // 2
    half_x, half_y = width_x // 2, width_y // 2
    quarter_x, quarter_y = width_x // 4, width_y // 4
    band = 2 * rows
    me = lax.axis_index("pencil")
    group = lax.axis_index("freq")
    core = lax.rem(me, 2)
    chip = lax.div(me, 2)
    partner = chip * 2 + (1 - core)

    per = rows // tile
    loads = {}
    for kind, (ref, buf) in enumerate(((wave_ref, wave_buf), (source_ref, source_buf))):
        for f in range(freqs):
            for c in range(2):
                src = ref.at[f, :, c, :] if kind == 0 else ref.at[0, f, :, c, :]
                copy = pltpu.make_async_copy(src, buf.at[f, c], load_sem.at[kind, f, c])
                copy.start()
                loads[kind, f, c] = copy

    tables = []
    for i, (ref, buf) in enumerate(
        ((high_x_ref, high_x), (low_x_ref, low_x), (high_back_ref, high_back), (low_back_ref, low_back))
    ):
        copy = pltpu.make_async_copy(ref, buf, table_sem.at[i])
        copy.start()
        tables.append(copy)

    barrier = pltpu.get_barrier_semaphore()
    for step in range(1, pencils):
        pl.semaphore_signal(
            barrier, inc=1, device_id=(group, lax.rem(me + step, pencils)), device_id_type=MESH
        )
    for step in range(1, groups):
        pl.semaphore_signal(
            barrier, inc=1, device_id=(lax.rem(group + step, groups), me), device_id_type=MESH
        )

    sends = []
    for f in range(freqs):
        for c in range(2):
            loads[0, f, c].wait()
            values = wave_buf[f, c]
            first, second = values[:, :half_y], values[:, half_y:]
            for flip in (1, 0):
                to_core = lax.rem(core + flip, 2)
                sign = jnp.where(to_core == 0, 1.0, -1.0)
                mixed = halves(first + sign * second)
                piece = product(mixed, (high_fwd[to_core], low_fwd[to_core]))
                stage[f, c, flip] = piece
                if flip == 0:
                    recv[f, me, c] = piece
                if f == 0 and c == 0 and flip == 1:
                    pl.semaphore_wait(barrier, pencils - 1 + groups - 1)
                for far in list(range(1, chips)) + [0]:
                    if far == 0 and flip == 0:
                        continue
                    slot = far * 2 + flip
                    target = lax.rem(chip + far, chips) * 2 + to_core
                    copy = pltpu.make_async_remote_copy(
                        src_ref=stage.at[f, c, flip],
                        dst_ref=recv.at[f, me, c],
                        send_sem=send_sem.at[f, c, slot],
                        recv_sem=recv_sem.at[f, c, slot],
                        device_id=(group, target),
                        device_id_type=MESH,
                    )
                    copy.start()
                    sends.append((f, c, copy))

    tile_rows = band // tile
    tiles_y = width_y // tile
    lane_y = lax.broadcasted_iota(jnp.int32, (8, width_y), 1)
    bases, offsets = [], []
    for t in range(tile_rows):
        owner = 1 - core if t < per else core
        row = chip * tile_rows + owner * per + t % per
        offsets.append(pl.multiple_of(owner * rows + (t % per) * tile, tile))
        lowers = [lower_ref[row, q] for q in range(tiles_y)]
        base = functools.reduce(jnp.minimum, lowers)
        base = jnp.minimum(base, refs - 3)
        bases.append(base)
        for k in range(3):
            line = jnp.zeros((8, width_y), jnp.float32)
            for q in range(tiles_y):
                w = weight_ref[row, q]
                value = jnp.where(lowers[q] == base + k, w, 0.0) + jnp.where(
                    lowers[q] + 1 == base + k, 1.0 - w, 0.0
                )
                line = jnp.where((lane_y >= q * tile) & (lane_y < (q + 1) * tile), value, line)
            coef[t, k] = line

    step_x = 2.0 * math.pi / (width_x * GRID_SPACING)
    step_y = 2.0 * math.pi / (width_y * GRID_SPACING)

    def terms(angular, velocity, radial):
        vertical = (angular / velocity) ** 2 - radial
        travel = jnp.sqrt(jnp.maximum(vertical, 0.0)) * DEPTH_STEP
        damping = jnp.exp(-jnp.sqrt(jnp.maximum(-vertical, 0.0)) * DEPTH_STEP)
        return damping * jnp.cos(travel), damping * jnp.sin(travel)

    lanes = lax.broadcasted_iota(jnp.int32, (1, quarter_y), 1)
    ky = (2 * lanes + core).astype(jnp.float32) * step_y
    ky_extra = jnp.where(core == 0, half_y, 1).astype(jnp.float32) * step_y
    even_rows = 2 * lax.broadcasted_iota(jnp.int32, (quarter_x, 1), 0)
    kx_even = even_rows.astype(jnp.float32) * step_x
    kx_odd = (even_rows + 1).astype(jnp.float32) * step_x
    kx_last = jnp.full((8, 1), half_x, jnp.int32).astype(jnp.float32) * step_x
    row_id = lax.broadcasted_iota(jnp.int32, (quarter_x, quarter_y), 0)
    lane_id = lax.broadcasted_iota(jnp.int32, (quarter_x, quarter_y), 1)
    speeds_row = jnp.full((1, quarter_y), speed_ref[0, 0], jnp.float32)
    for r in range(1, refs):
        speeds_row = jnp.where(lanes == r, speed_ref[0, r], speeds_row)

    for f in range(freqs):
        angular = omega_ref[f]
        extra = [
            terms(angular, speeds_row, kx * kx + ky_extra * ky_extra)
            for kx in (kx_even, kx_last, kx_odd)
        ]
        for r in range(refs):
            velocity = speed_ref[0, r]
            main = [
                terms(angular, velocity, kx * kx + ky * ky) for kx in (kx_even, kx_last, kx_odd)
            ]
            for part in range(2):
                even, last, odd = (m[part] for m in main)
                even_x, last_x, odd_x = (m[part][:, r : r + 1] for m in extra)
                even_s = jnp.where(row_id == 0, last[0:1], even)
                even_sx = jnp.where(row_id[:, 0:1] == 0, last_x[0:1], even_x)
                blocks = ((even, even_x), (even_s, even_sx), (odd, odd_x), (odd, odd_x))
                for i, (block, column) in enumerate(blocks):
                    span = slice(i * quarter_x, (i + 1) * quarter_x)
                    phase[f, r, part, span, :quarter_y] = block
                    phase[f, r, part, span, quarter_y:] = jnp.where(lane_id == 0, column, block)

    for copy in tables:
        copy.wait()
    start = lax.rem(chip * band, half_x)
    sign_x = jnp.where(chip * band < half_x, 1.0, -1.0)
    sign_y = jnp.where(core == 0, 1.0, -1.0)
    start = pl.multiple_of(start, rows)
    back = [
        (high_x[1, e, pl.ds(start, band), :], low_x[1, e, pl.ds(start, band), :]) for e in range(2)
    ]
    table_y = (high_back[core], low_back[core])

    own_width = width_y // groups
    packs = 128 // own_width
    chunk = tile // packs
    lane = lax.broadcasted_iota(jnp.int32, (chunk, 128), 1)
    pair_copies, stores, image_copies = [], [], []

    def finish(f):
        last = f == freqs - 1
        for i in range(per):
            span = slice(i * tile, (i + 1) * tile)
            pair_copies[f * per + i].wait_recv()
            image = None
            for c in range(2):
                value = blend_own[f, c, span] + blend_recv[f, i, c]
                out_buf[f, c, span] = value
                if i == 0:
                    loads[1, f, c].wait()
                term = source_buf[f, c, span] * value
                image = term if image is None else image + term
            if f > 0:
                image = image + img_acc[span]
            if not last:
                img_acc[span] = image
                continue
            image = image * scale
            for g in range(groups):
                at = g * own_width
                column = image[:, at // 128 * 128 : at // 128 * 128 + 128]
                packed = None
                for j in range(packs):
                    part = column[j * chunk : (j + 1) * chunk]
                    shift = (j * own_width - at) % 128
                    if shift:
                        part = pltpu.roll(part, shift, 1)
                    packed = part if packed is None else jnp.where(lane >= j * own_width, part, packed)
                img_send[i, g] = packed
            for step in range(1, groups):
                to = lax.rem(group + step, groups)
                copy = pltpu.make_async_remote_copy(
                    src_ref=img_send.at[i, to],
                    dst_ref=img_recv.at[i, step],
                    send_sem=isend_sem.at[i, step],
                    recv_sem=irecv_sem.at[i, step],
                    device_id=(to, me),
                    device_id_type=MESH,
                )
                copy.start()
                image_copies.append((i, step, copy))
        for c in range(2):
            copy = pltpu.make_async_copy(out_buf.at[f, c], out_ref.at[f, :, c, :], store_sem.at[f, c])
            copy.start()
            stores.append(copy)

    for f in range(freqs):
        if f > 0:
            finish(f - 1)
        spectrum = []
        for c in range(2):
            for g, d, copy in sends:
                if (g, d) == (f, c):
                    copy.wait_recv()
            upper = recv[f, 0 : pencils // 2, c].reshape(half_x, half_y)
            lower = recv[f, pencils // 2 : pencils, c].reshape(half_x, half_y)
            even = product((high_x[0, 0], low_x[0, 0]), halves(upper + lower))
            odd = product((high_x[0, 1], low_x[0, 1]), halves(upper - lower))
            spectrum.append((even, odd))

        def one_ref(r, carry):
            total = [None, None]
            for e in range(2):
                span = slice(e * half_x, (e + 1) * half_x)
                real, imag = spectrum[0][e], spectrum[1][e]
                pc, ps = phase[f, r, 0, span, :], phase[f, r, 1, span, :]
                moved = (real * pc - imag * ps, real * ps + imag * pc)
                for c in range(2):
                    share = product(back[e], halves(moved[c]))
                    total[c] = share if e == 0 else total[c] + sign_x * share
            for c in range(2):
                shifted[r, c] = total[c]
            return carry

        for r in range(refs):
            one_ref(r, 0)

        for t in range(tile_rows):
            lo, hi = [None, None], [None, None]
            for k in range(3):
                block = shifted[bases[t] + k, :, pl.ds(offsets[t], tile), :]
                space = product(halves(block.reshape(2 * tile, half_y)), table_y)
                for c in range(2):
                    piece = space[c * tile : (c + 1) * tile]
                    a = coef[t, k, 0:1, :half_y] * piece
                    b = coef[t, k, 0:1, half_y:] * piece
                    lo[c] = a if k == 0 else lo[c] + a
                    hi[c] = b if k == 0 else hi[c] + b
            inner = (t % per) * tile
            for c in range(2):
                if t < per:
                    blend_send[f, t, c, :, :half_y] = lo[c]
                    blend_send[f, t, c, :, half_y:] = hi[c] * sign_y
                else:
                    blend_own[f, c, inner : inner + tile, :half_y] = lo[c]
                    blend_own[f, c, inner : inner + tile, half_y:] = hi[c] * sign_y
            if t < per:
                copy = pltpu.make_async_remote_copy(
                    src_ref=blend_send.at[f, t],
                    dst_ref=blend_recv.at[f, t],
                    send_sem=pair_send.at[f, t],
                    recv_sem=pair_recv.at[f, t],
                    device_id=(group, partner),
                    device_id_type=MESH,
                )
                copy.start()
                pair_copies.append(copy)
    finish(freqs - 1)

    lines = []
    for i in range(per):
        total = img_send[i, group]
        for j, step, copy in image_copies:
            if j == i:
                copy.wait_recv()
                total = total + img_recv[i, step]
        for j in range(packs):
            part = pltpu.roll(total, (-j * own_width) % 128, 1) if j else total
            lines.append(part[:, :own_width])
    image_ref[...] = jnp.concatenate(lines, axis=0).T

    for copy in stores:
        copy.wait()
    for _, _, copy in sends:
        copy.wait_send()
    for copy in pair_copies:
        copy.wait_send()
    for _, _, copy in image_copies:
        copy.wait_send()


def settle(from_field, from_image, field, image, sem, image_sem):
    freqs, rows = field.shape[:2]
    parts = 4
    step = rows // parts
    copies = [pltpu.make_async_copy(from_image, image, image_sem)]
    for f in range(freqs):
        for i in range(parts):
            span = pl.ds(i * step, step)
            copies.append(
                pltpu.make_async_copy(from_field.at[f, span], field.at[f, span], sem.at[f, i])
            )
    for copy in copies:
        copy.start()
    for copy in copies:
        copy.wait()


def on_device(wave_field, source_field, omegas, velocities, lower_ref, blend_weight):
    pencils = lax.axis_size("pencil")
    groups = lax.axis_size("freq")
    freqs, rows, _, width_y = wave_field.shape
    width_x = rows * pencils
    refs = velocities.shape[1]
    tile = width_x // lower_ref.shape[1]
    half_y = width_y // 2
    scale = 1.0 / math.sqrt(freqs * groups)
    dims = (freqs, pencils, groups, rows, width_x, width_y, refs, tile, scale)
    own_width = width_y // groups
    high_x, low_x = real_tables(width_x)
    high_y, low_y = real_tables(width_y)
    tables = [jnp.asarray(t) for t in (high_y[1], low_y[1], high_x, low_x, high_y[0], low_y[0])]
    hbm = pl.BlockSpec(memory_space=pl.ANY)
    vmem = pl.BlockSpec(memory_space=pltpu.VMEM)
    smem = pl.BlockSpec(memory_space=pltpu.SMEM)
    f32 = jnp.float32
    per = rows // tile
    packed = (per, groups, tile * own_width // 128, 128)
    out, image = pl.pallas_call(
        functools.partial(kernel, dims),
        out_shape=(
            jax.ShapeDtypeStruct(wave_field.shape, f32),
            jax.ShapeDtypeStruct((own_width, rows), f32),
        ),
        in_specs=[hbm] * 2 + [vmem] * 2 + [hbm] * 4 + [smem] * 4,
        out_specs=(hbm, vmem),
        scratch_shapes=[
            pltpu.VMEM((freqs, 2, 2, rows, half_y), f32),
            pltpu.VMEM((freqs, pencils, 2, rows, half_y), f32),
            pltpu.VMEM((freqs, refs, 2, width_x, half_y), f32),
            pltpu.VMEM((refs, 2, 2 * rows, half_y), f32),
            pltpu.VMEM((2 * per, 3, 8, width_y), f32),
            pltpu.VMEM((freqs, 2, rows, width_y), f32),
            pltpu.VMEM((freqs, per, 2, tile, width_y), f32),
            pltpu.VMEM((freqs, per, 2, tile, width_y), f32),
            pltpu.VMEM((rows, width_y), f32),
            pltpu.VMEM(packed, f32),
            pltpu.VMEM(packed, f32),
            pltpu.VMEM((freqs, 2, rows, width_y), f32),
            pltpu.VMEM((freqs, 2, rows, width_y), f32),
            pltpu.VMEM((freqs, 2, rows, width_y), f32),
            pltpu.VMEM(high_x.shape, jnp.bfloat16),
            pltpu.VMEM(high_x.shape, jnp.bfloat16),
            pltpu.VMEM(high_y.shape[1:], jnp.bfloat16),
            pltpu.VMEM(high_y.shape[1:], jnp.bfloat16),
            pltpu.SemaphoreType.DMA((4,)),
            pltpu.SemaphoreType.DMA((2, freqs, 2)),
            pltpu.SemaphoreType.DMA((freqs, 2)),
            pltpu.SemaphoreType.DMA((freqs, 2, pencils)),
            pltpu.SemaphoreType.DMA((freqs, 2, pencils)),
            pltpu.SemaphoreType.DMA((freqs, per)),
            pltpu.SemaphoreType.DMA((freqs, per)),
            pltpu.SemaphoreType.DMA((per, groups)),
            pltpu.SemaphoreType.DMA((per, groups)),
        ],
        compiler_params=pltpu.CompilerParams(
            collective_id=0, has_side_effects=True, vmem_limit_bytes=56 * 1024 * 1024
        ),
    )(wave_field, source_field, *tables, omegas, velocities, lower_ref[0], blend_weight[0])
    out, image = pl.pallas_call(
        settle,
        out_shape=(
            jax.ShapeDtypeStruct(out.shape, f32),
            jax.ShapeDtypeStruct(image.shape, f32),
        ),
        in_specs=[hbm, hbm],
        out_specs=(hbm, hbm),
        scratch_shapes=[pltpu.SemaphoreType.DMA((freqs, 4)), pltpu.SemaphoreType.DMA],
        compiler_params=pltpu.CompilerParams(has_side_effects=True),
    )(out, image)
    return out, image.T[None]


def solution(mesh):
    placed = (
        P("freq", "pencil", None, None),
        P(None, "freq", "pencil", None, None),
        P("freq"),
        P(),
        P(),
        P(),
    )
    return jax.shard_map(
        on_device,
        mesh=mesh,
        in_specs=placed,
        out_specs=(P("freq", "pencil", None, None), P(None, "pencil", "freq")),
        check_vma=False,
    )
```
